1024 devices in a mesh: group: 64 (over z_hi, y, core), shard: 16 (over z_lo, x).
Axes of the slice: x: 8, y: 8, z: 8 (z_hi: 4, z_lo: 2; z = z_hi * 2 + z_lo), core: 2. Of those that a mesh axis runs over, the one named last changes fastest.
Arguments:
- tokens: bfloat16 [20480, 3072], P(('group', 'shard')), may hold values from -6 to 6
- route_weight: bfloat16 [20480], P(('group', 'shard')), may hold values from 0.099609375 to 1
- counts: int32 [64], P('group'), may hold values from 80 to 320, as said below
- pulled: int32 [64], replicated, may hold values from 0 to 15
- weights: bfloat16 [16, 3072, 5376], P(None, 'group', 'shard'), may hold values from -0.109375 to 0.109375
- cotangent: bfloat16 [20480, 5376], P('group', 'shard'), may hold values from -6 to 6
Outputs:
- activated: bfloat16 [20480, 5376], P('group', 'shard')
- input_grads: bfloat16 [20480, 3072], P(('group', 'shard'))
- weight_grads: float32 [16, 3072, 5376], P(None, 'group', 'shard')
The draws below stay inside these ranges and needn't reach their ends.
Inputs may be any that keep to these rules, and one draw needn't show every extreme that they name: `counts`: every draw has some group with all 320 slots live.
All inputs are finite; a program needn't handle non-finite values.
Results may differ from the reference program's by a relative error of at most 0.019.
Values may be sent and summed in bfloat16 or wider, within the bound.
A program may use at most 32 MiB of HBM per device.

```python
import math
import jax
import jax.numpy as jnp
import numpy as np
from jax import lax

D = 3072
FF = 5376
E = 16
CAP = 320
TOKENS = 20480
N_GROUP = 64
N_SHARD = 16


def draw_counts(key, part):
    key = jax.random.fold_in(key, 7)
    first, second = jax.random.split(key)
    values = jax.random.randint(first, (N_GROUP,), CAP // 4, CAP + 1)
    where_full = jax.random.randint(second, (), 0, N_GROUP)
    return values.at[where_full].set(CAP).astype(jnp.int32)


def with_ends(values, stream_key, low, high):
    index_at = [jax.random.randint(jax.random.fold_in(stream_key, axis), (), 0, length) for axis, length in enumerate(values.shape)]
    widest = values.shape.index(max(values.shape))
    next_to = index_at[:widest] + [(index_at[widest] + 1) % values.shape[widest]] + index_at[widest + 1:]
    return values.at[tuple(index_at)].set(low).at[tuple(next_to)].set(high)


def steps_of(own_key, shape, pieces, low, high):
    level = 1.0
    for axis_at, shards_of in pieces:
        heights = jax.random.uniform(jax.random.fold_in(jax.random.fold_in(own_key, 6), axis_at), (shards_of,), jnp.float32, low / len(pieces), high / len(pieces))
        level = level * jnp.repeat(jnp.exp(heights), shape[axis_at] // shards_of).reshape((-1,) + (1,) * (len(shape) - 1 - axis_at))
    return level


def rank_bounds(number_of, lean):
    loads = [(1 << 20) // math.isqrt(rank ** lean) + 1 for rank in range(1, number_of + 1)]
    width = 1 + sum(loads) // (1 << 30)
    return np.cumsum(np.array([max(1, weight // width) for weight in loads]))


def ranked_ids(stream_key, dims, number_of, slope):
    table = rank_bounds(number_of, slope)
    ticket = jax.random.randint(jax.random.fold_in(stream_key, 1), dims, 0, int(table[number_of - 1]))
    standing = jnp.searchsorted(jnp.asarray(table, jnp.int32), ticket, side="right")
    return jax.random.permutation(jax.random.fold_in(stream_key, 2), number_of)[standing].astype(jnp.int32)


def scatter_about(rng, dims, spread, reach, cuts=(), kind=jnp.bfloat16):
    entries = spread * jax.random.normal(rng, dims, jnp.float32)
    if cuts:
        entries = entries * steps_of(rng, dims, cuts, -0.22, 0.18)
    return jnp.clip(entries, -reach, reach).astype(kind)


def setup_inputs(seed: int = 0) -> dict:
    splits = jax.random.split(jax.random.key(seed), 7)
    return {
        "tokens": scatter_about(splits[0], (TOKENS, D), 1.0, 6.0, ((0, 1024),)),
        "route_weight": jnp.clip(jnp.exp(math.log(1.0) - 2.306499 * jax.random.uniform(splits[1], (TOKENS,), jnp.float32) ** steps_of(splits[1], (TOKENS,), ((0, 1024),), -0.2, 0.2)), 0.099609375, 1.0).astype(jnp.bfloat16),
        "counts": draw_counts(jax.random.fold_in(splits[6], 71), 0),
        "pulled": with_ends(ranked_ids(splits[3], (N_GROUP,), E, 2), jax.random.fold_in(splits[3], 3), 0, E - 1).astype(jnp.int32),
        "weights": scatter_about(splits[4], (E, D, FF), D ** -0.5, 0.109375, ((1, 64), (2, 16))),
        "cotangent": scatter_about(splits[5], (TOKENS, FF), 1.0, 6.0, ((0, 64), (1, 16))),
    }


def silu_parts(hidden):
    sigma = jax.nn.sigmoid(hidden)
    return hidden * sigma, sigma * (1.0 + hidden * (1.0 - sigma))


def reference(tokens, route_weight, counts, pulled, weights, cotangent):
    tok_groups = tokens.reshape(N_GROUP, CAP, D)
    route_groups = route_weight.reshape(N_GROUP, CAP)
    cot_groups = cotangent.reshape(N_GROUP, CAP, FF)
    width_block = FF // N_SHARD

    def step(gradient, inputs):
        tok_rows, route_rows, live_count, expert, cot_rows = inputs
        expert_weight = lax.dynamic_index_in_dim(weights, expert.astype(jnp.int32), 0, keepdims=False)
        hidden = jnp.dot(tok_rows, expert_weight, preferred_element_type=jnp.float32)
        valid_rows = jnp.arange(CAP, dtype=jnp.int32) < live_count.astype(jnp.int32)
        weighting = jnp.where(valid_rows, route_rows.astype(jnp.float32), jnp.float32(0.0))[:, None]
        activated, derivative = silu_parts(hidden)
        output = (weighting * activated).astype(jnp.bfloat16)
        back_signal = (cot_rows.astype(jnp.float32) * weighting * derivative).astype(jnp.bfloat16)
        total = jnp.zeros((CAP, D), jnp.float32)
        for column_block in range(N_SHARD):
            lower = column_block * width_block
            term = jnp.dot(back_signal[:, lower:lower + width_block], expert_weight[:, lower:lower + width_block].T, preferred_element_type=jnp.float32)
            term = lax.optimization_barrier(term.astype(jnp.bfloat16))
            total = total + term.astype(jnp.float32)
        input_part = total.astype(jnp.bfloat16)
        partial_value = jnp.dot(tok_rows.T, back_signal, preferred_element_type=jnp.float32).astype(jnp.bfloat16)
        partial_value = lax.optimization_barrier(partial_value)
        gradient = gradient.at[expert.astype(jnp.int32)].add(partial_value.astype(jnp.float32))
        return gradient, (output, input_part)

    start = jnp.zeros((E, D, FF), jnp.float32)
    gradient, (outputs, input_parts) = lax.scan(step, start, (tok_groups, route_groups, counts, pulled, cot_groups))
    return outputs.reshape(TOKENS, FF), input_parts.reshape(TOKENS, D), gradient
```

```python
import functools

import jax
import jax.numpy as jnp
from jax import lax
from jax.experimental import pallas as pl
from jax.experimental.pallas import tpu as pltpu
from jax.sharding import PartitionSpec as P

MESH = pl.DeviceIdType.MESH
NZ, NY, NC, NX = 4, 8, 2, 8
ROWS, COLS, TOK = 48, 336, 20
CAP, D = 320, 3072
KC = 8
KW = D // KC
BF, F32 = jnp.bfloat16, jnp.float32
ORDER_Y = (1, 7, 2, 6, 3, 5, 4)
ORDER_Z = (1, 3, 2)


def pack(wide):
    n = wide.shape[0]
    tail = wide[:, :, 256:]
    lane = lax.broadcasted_iota(jnp.int32, (n, 16, 128), 2)
    last = tail[:, 32:48]
    low = jnp.where(lane < 80, tail[:, 0:16], pltpu.roll(last, 80, 2))
    high = jnp.where(lane < 80, tail[:, 16:32], pltpu.roll(last, 32, 2))
    return jnp.concatenate([wide[:, :, 0:128], wide[:, :, 128:256], low, high], axis=1)


def unpack_tail(tail):
    n = tail.shape[0]
    lane = lax.broadcasted_iota(jnp.int32, (n, 16, 128), 2)
    zero = jnp.zeros((n, 16, 128), F32)
    low, high = tail[:, 0:16], tail[:, 16:32]
    last = jnp.where(lane < 48, pltpu.roll(low, 48, 2), jnp.where(lane < 80, pltpu.roll(high, 96, 2), zero))
    return jnp.concatenate([jnp.where(lane < 80, low, zero), jnp.where(lane < 80, high, zero), last], axis=1)


def main_kernel(
    pulled, counts, tok, route, weights, cot,
    act_out, dx_out, grad_out,
    packed, send_a, send_b, mid_a, mid_b, land, full,
    back_a, back_b, bmid_a, bmid_b,
    own_tok, pair_tok, ring, xk, xt, scale, cotp, hid, sig,
    terms, got, zsend, zrecv, half,
    w1a, w1b, w2, wl, g1a, g1b, g2, gl, ps, rg, xs,
):
    g, s = lax.axis_index("group"), lax.axis_index("shard")
    zh, y, c = g // 16, lax.rem(g // 2, NY), lax.rem(g, 2)
    zl, x = s // NX, lax.rem(s, NX)

    def gdev(zh_, y_, c_):
        return ((zh_ * NY + y_) * 2 + c_, s)

    def sdev(zl_, x_):
        return (g, zl_ * NX + x_)

    bar = pltpu.get_barrier_semaphore()

    def greet(dev):
        pl.semaphore_signal(bar, inc=1, device_id=dev, device_id_type=MESH)

    for dy in range(1, NY):
        greet(gdev(zh, lax.rem(y + dy, NY), c))
        greet(gdev(zh, lax.rem(y + dy, NY), 1 - c))
    for dz in range(1, NZ):
        greet(gdev(lax.rem(zh + dz, NZ), y, c))
        greet(gdev(lax.rem(zh + dz, NZ), y, 1 - c))
    greet(gdev(zh, y, 1 - c))
    for dx in range(1, NX):
        greet(sdev(zl, lax.rem(x + dx, NX)))
    greet(sdev(1 - zl, x))

    own_tok[:, 0:D] = tok[...]
    own_tok[:, D:] = route[...]

    def pack_one(e, carry):
        wide = jnp.concatenate([weights[e].astype(F32), jnp.zeros((ROWS, 384 - COLS), F32)], axis=1)
        packed[e] = pack(wide[None])[0].astype(BF)
        return carry

    lax.fori_loop(0, weights.shape[0], pack_one, 0)

    def fill(k, carry):
        zt, yt = k // NY, lax.rem(k, NY)
        send_a[yt, zt] = packed[pulled[2 * k]]
        send_b[zt, yt] = packed[pulled[2 * k + 1]]
        return carry

    lax.fori_loop(0, NZ * NY, fill, 0)

    pl.semaphore_wait(bar, 29)

    def exchange(src_a, src_b, ia, ib, dst, s1a, s1b, s2, sl):
        def a1(dy):
            yt = lax.rem(y + dy, NY)
            return pltpu.make_async_remote_copy(
                src_a.at[yt], ia.at[y], s1a.at[0, dy], s1a.at[1, dy], device_id=gdev(zh, yt, c), device_id_type=MESH)

        def b1(dz):
            zt = lax.rem(zh + dz, NZ)
            return pltpu.make_async_remote_copy(
                src_b.at[zt], ib.at[zh], s1b.at[0, dz], s1b.at[1, dz], device_id=gdev(zt, y, c), device_id_type=MESH)

        def a2(dz, cross):
            zt = lax.rem(zh + dz, NZ)
            k = dz * 2 + cross
            return pltpu.make_async_remote_copy(
                ia.at[:, zt], dst.at[zh, :, c], s2.at[0, k], s2.at[1, k], device_id=gdev(zt, y, 0), device_id_type=MESH)

        def b2(dy, cross):
            yt = lax.rem(y + dy, NY)
            k = dy * 2 + cross
            return pltpu.make_async_remote_copy(
                ib.at[:, yt], dst.at[:, y, c], s2.at[0, k], s2.at[1, k], device_id=gdev(zh, yt, 1), device_id_type=MESH)

        la = pltpu.make_async_copy(src_a.at[y], ia.at[y], sl.at[0])
        lb = pltpu.make_async_copy(src_b.at[zh], ib.at[zh], sl.at[1])
        l2a = pltpu.make_async_copy(ia.at[:, zh], dst.at[zh, :, 0], sl.at[2])
        l2b = pltpu.make_async_copy(ib.at[:, y], dst.at[:, y, 1], sl.at[2])

        def start1():
            la.start()
            lb.start()
            for i, dy in enumerate(ORDER_Y):
                a1(dy).start()
                if i % 2 == 0 and i // 2 < 3:
                    b1(ORDER_Z[i // 2]).start()

        def turn_a():
            la.wait()
            for dy in ORDER_Y:
                a1(dy).wait()

            @pl.when(c == 0)
            def _():
                l2a.start()
                for dz in ORDER_Z:
                    a2(dz, 0).start()

            @pl.when(c == 1)
            def _():
                for dz in ORDER_Z + (0,):
                    a2(dz, 1).start()

        def turn_b():
            lb.wait()
            for dz in ORDER_Z:
                b1(dz).wait()

            @pl.when(c == 1)
            def _():
                l2b.start()
                for dy in ORDER_Y:
                    b2(dy, 0).start()

            @pl.when(c == 0)
            def _():
                for dy in ORDER_Y + (0,):
                    b2(dy, 1).start()

        def finish():
            @pl.when(c == 0)
            def _():
                l2a.wait()
                for dz in ORDER_Z:
                    a2(dz, 0).wait()
                for dz in ORDER_Z + (0,):
                    a2(dz, 1).wait_recv()
                for dy in ORDER_Y + (0,):
                    b2(dy, 1).wait_send()

            @pl.when(c == 1)
            def _():
                l2b.wait()
                for dy in ORDER_Y:
                    b2(dy, 0).wait()
                for dy in ORDER_Y + (0,):
                    b2(dy, 1).wait_recv()
                for dz in ORDER_Z + (0,):
                    a2(dz, 1).wait_send()

        return start1, turn_a, turn_b, finish

    pair = pltpu.make_async_remote_copy(
        own_tok, pair_tok, ps.at[0], ps.at[1], device_id=sdev(1 - zl, x), device_id_type=MESH)
    pair.start()
    w_start1, w_turn_a, w_turn_b, w_finish = exchange(
        send_a, send_b, mid_a, mid_b, land, w1a, w1b, w2, wl)
    w_start1()

    pair.wait()
    mine, other = own_tok[...].astype(F32), pair_tok[...].astype(F32)
    ring[x] = jnp.concatenate(
        [jnp.where(zl == 0, mine, other), jnp.where(zl == 0, other, mine)], axis=0).astype(BF)

    right, left = lax.rem(x + 1, NX), lax.rem(x + NX - 1, NX)
    cut = 13 * 128

    def hop(step):
        a, b = lax.rem(x - step + 1 + NX, NX), lax.rem(x + step - 1, NX)
        if step < 4:
            ra, rb = ring.at[a], ring.at[b]
        else:
            ra, rb = ring.at[a, :, 0:cut], ring.at[b, :, cut:]
        k = 2 * (step - 1)
        return (
            pltpu.make_async_remote_copy(
                ra, ra, rg.at[0, k], rg.at[1, k], device_id=sdev(zl, right), device_id_type=MESH),
            pltpu.make_async_remote_copy(
                rb, rb, rg.at[0, k + 1], rg.at[1, k + 1], device_id=sdev(zl, left), device_id_type=MESH),
        )

    def hop_start(step):
        for copy in hop(step):
            copy.start()

    def hop_wait(step):
        for copy in hop(step):
            copy.wait()

    hop_start(1)
    cotp[:, 256:] = jnp.zeros((CAP, 128), F32)
    cotp[:, 0:COLS] = cot[...].astype(F32)
    hop_wait(1)
    hop_start(2)
    hop_wait(2)
    hop_start(3)
    w_turn_a()
    w_turn_b()
    hop_wait(3)
    hop_start(4)
    hop_wait(4)

    def gather_rows(lanes):
        parts = [ring[i, :, lanes].astype(F32) for i in range(NX)]
        return jnp.concatenate([p[0:TOK] for p in parts] + [p[TOK:] for p in parts], axis=0)

    def order(k, carry):
        rows = gather_rows(pl.ds(pl.multiple_of(k * KW, 128), KW))
        xk[k] = rows.astype(BF)
        xt[k] = rows.T.astype(BF)
        return carry

    lax.fori_loop(0, KC, order, 0)
    live = lax.broadcasted_iota(jnp.int32, (CAP, 128), 0) < counts[0]
    scale[...] = jnp.where(live, gather_rows(pl.ds(D, 128)), jnp.zeros((CAP, 128), F32))
    hid[...] = jnp.zeros((CAP, 384), F32)

    w_finish()

    def forward(k, carry):
        blocks = land[k // 2, pl.ds(lax.rem(k, 2) * 4, 4)].reshape(8, 128, 128)
        tail = unpack_tail(blocks[:, 96:].astype(F32)).reshape(KW, 128).astype(BF)
        chunk = jnp.concatenate(
            [blocks[:, 0:ROWS].reshape(KW, 128), blocks[:, ROWS:2 * ROWS].reshape(KW, 128), tail], axis=1)
        full[k] = chunk
        hid[...] += jnp.dot(xk[k], chunk, preferred_element_type=F32)
        return carry

    lax.fori_loop(0, KC, forward, 0)

    for t in range(3):
        lanes = slice(128 * t, 128 * t + 128)
        h, sc = hid[:, lanes], scale[...]
        sigma = jax.nn.sigmoid(h)
        value = (sc * (h * sigma)).astype(BF)
        if t < 2:
            act_out[:, lanes] = value
        else:
            act_out[:, 256:COLS] = value[:, 0:80]
        sig[:, lanes] = (cotp[:, lanes] * sc * (sigma * (1.0 + h * (1.0 - sigma)))).astype(BF)

    def grads(k, carry):
        part = jnp.dot(xt[k], sig[...], preferred_element_type=F32)
        blocks = pack(part.reshape(8, ROWS, 384)).astype(BF)
        zt, y0 = k // 2, lax.rem(k, 2) * 4
        for j in range(4):
            back_a[y0 + j, zt] = blocks[2 * j]
            back_b[zt, y0 + j] = blocks[2 * j + 1]
        return carry

    lax.fori_loop(0, KC, grads, 0)
    g_start1, g_turn_a, g_turn_b, g_finish = exchange(
        back_a, back_b, bmid_a, bmid_b, grad_out, g1a, g1b, g2, gl)
    g_start1()

    def inputs(k, carry):
        term = lax.dot_general(sig[...], full[k], (((1,), (1,)), ((), ())), preferred_element_type=F32)
        lanes = pl.ds(pl.multiple_of(k * KW, 128), KW)
        for i in range(NX):
            terms[i, :, lanes] = jnp.concatenate(
                [term[TOK * i:TOK * i + TOK], term[160 + TOK * i:160 + TOK * i + TOK]], axis=0).astype(BF)
        return carry

    lax.fori_loop(0, KC, inputs, 0)

    def xcopy(dx):
        xt_ = lax.rem(x + dx, NX)
        return pltpu.make_async_remote_copy(
            terms.at[xt_], got.at[x], xs.at[0, dx], xs.at[1, dx], device_id=sdev(zl, xt_), device_id_type=MESH)

    for dx in ORDER_Y:
        xcopy(dx).start()
    got[x] = terms[x]

    g_turn_a()
    g_turn_b()
    for dx in ORDER_Y:
        xcopy(dx).wait()

    def add_up(k, carry):
        lanes = pl.ds(pl.multiple_of(k * KW, 128), KW)
        total = got[0, :, lanes].astype(F32)
        for i in range(1, NX):
            total = total + got[i, :, lanes].astype(F32)
        low, high = total[0:TOK], total[TOK:]
        half[:, lanes] = jnp.where(zl == 0, low, high)
        zsend[:, lanes] = jnp.where(zl == 0, high, low).astype(BF)
        return carry

    lax.fori_loop(0, KC, add_up, 0)
    last = pltpu.make_async_remote_copy(
        zsend, zrecv, ps.at[2], ps.at[3], device_id=sdev(1 - zl, x), device_id_type=MESH)
    last.start()
    last.wait()
    dx_out[...] = (half[...] + zrecv[...].astype(F32)).astype(BF)
    g_finish()


def sum_kernel(pulled, blocks, out, acc):
    acc[...] = jnp.zeros(acc.shape, F32)

    def add(k, carry):
        e = pulled[k]
        acc[e] = acc[e] + blocks[k].astype(F32)
        return carry

    lax.fori_loop(0, blocks.shape[0], add, 0)

    def spread(e, carry):
        total = acc[e]
        out[e, :, 0:128] = total[0:ROWS]
        out[e, :, 128:256] = total[ROWS:2 * ROWS]
        out[e, :, 256:COLS] = unpack_tail(total[None, 96:])[0, :, 0:80]
        return carry

    lax.fori_loop(0, out.shape[0], spread, 0)


def shards(tokens, route_weight, counts, pulled, weights, cotangent):
    vmem, smem = pl.BlockSpec(memory_space=pltpu.VMEM), pl.BlockSpec(memory_space=pltpu.SMEM)
    dma = pltpu.SemaphoreType.DMA
    route = jnp.broadcast_to(route_weight[:, None], (TOK, 128))
    activated, input_grads, blocks = pl.pallas_call(
        main_kernel,
        out_shape=[
            jax.ShapeDtypeStruct((CAP, COLS), BF),
            jax.ShapeDtypeStruct((TOK, D), BF),
            jax.ShapeDtypeStruct((NZ, NY, NC, 128, 128), BF),
        ],
        in_specs=[smem, smem, vmem, vmem, vmem, vmem],
        out_specs=[vmem, vmem, vmem],
        scratch_shapes=[
            pltpu.VMEM((16, 128, 128), BF),
            pltpu.VMEM((NY, NZ, 128, 128), BF),
            pltpu.VMEM((NZ, NY, 128, 128), BF),
            pltpu.VMEM((NY, NZ, 128, 128), BF),
            pltpu.VMEM((NZ, NY, 128, 128), BF),
            pltpu.VMEM((NZ, NY, NC, 128, 128), BF),
            pltpu.VMEM((KC, KW, 384), BF),
            pltpu.VMEM((NY, NZ, 128, 128), BF),
            pltpu.VMEM((NZ, NY, 128, 128), BF),
            pltpu.VMEM((NY, NZ, 128, 128), BF),
            pltpu.VMEM((NZ, NY, 128, 128), BF),
            pltpu.VMEM((TOK, D + 128), BF),
            pltpu.VMEM((TOK, D + 128), BF),
            pltpu.VMEM((NX, 2 * TOK, D + 128), BF),
            pltpu.VMEM((KC, CAP, KW), BF),
            pltpu.VMEM((KC, KW, CAP), BF),
            pltpu.VMEM((CAP, 128), F32),
            pltpu.VMEM((CAP, 384), F32),
            pltpu.VMEM((CAP, 384), F32),
            pltpu.VMEM((CAP, 384), BF),
            pltpu.VMEM((NX, 2 * TOK, D), BF),
            pltpu.VMEM((NX, 2 * TOK, D), BF),
            pltpu.VMEM((TOK, D), BF),
            pltpu.VMEM((TOK, D), BF),
            pltpu.VMEM((TOK, D), F32),
            dma((2, NY)), dma((2, NZ)), dma((2, 2 * NY)), dma((3,)),
            dma((2, NY)), dma((2, NZ)), dma((2, 2 * NY)), dma((3,)),
            dma((4,)), dma((2, 8)), dma((2, NX)),
        ],
        compiler_params=pltpu.CompilerParams(
            collective_id=1, has_side_effects=True, vmem_limit_bytes=50 << 20),
        name="exchange_and_compute",
    )(pulled, counts, tokens, route, weights, cotangent)
    weight_grads = pl.pallas_call(
        sum_kernel,
        out_shape=jax.ShapeDtypeStruct(weights.shape, F32),
        in_specs=[smem, vmem],
        out_specs=vmem,
        scratch_shapes=[pltpu.VMEM((weights.shape[0], 128, 128), F32)],
        compiler_params=pltpu.CompilerParams(vmem_limit_bytes=24 << 20),
        name="sum_per_expert",
    )(pulled, blocks.reshape(NZ * NY * NC, 128, 128))
    return activated, input_grads, weight_grads


def solution(mesh):
    in_specs = (
        P(("group", "shard"), None),
        P(("group", "shard")),
        P("group"),
        P(),
        P(None, "group", "shard"),
        P("group", "shard"),
    )
    out_specs = (P("group", "shard"), P(("group", "shard"), None), P(None, "group", "shard"))
    return jax.shard_map(shards, mesh=mesh, in_specs=in_specs, out_specs=out_specs, check_vma=False)
```

```python
import functools

import jax
import jax.numpy as jnp
from jax import lax
from jax.experimental import pallas as pl
from jax.experimental.pallas import tpu as pltpu
from jax.sharding import PartitionSpec as P

MESH = pl.DeviceIdType.MESH
NZ, NY, NC, NX = 4, 8, 2, 8
ROWS, COLS, TOK = 48, 336, 20
CAP, D = 320, 3072
KC = 8
KW = D // KC
BF, F32 = jnp.bfloat16, jnp.float32
ORDER_Y = (1, 7, 2, 6, 3, 5, 4)
ORDER_Z = (1, 3, 2)


def pack_tail(tail):
    n = tail.shape[0]
    lane = lax.broadcasted_iota(jnp.int32, (n, 16, 128), 2)
    last = tail[:, 32:48]
    low = jnp.where(lane < 80, tail[:, 0:16], pltpu.roll(last, 80, 2))
    high = jnp.where(lane < 80, tail[:, 16:32], pltpu.roll(last, 32, 2))
    return jnp.concatenate([low, high], axis=1)


def unpack_tail(tail):
    n = tail.shape[0]
    lane = lax.broadcasted_iota(jnp.int32, (n, 16, 128), 2)
    zero = jnp.zeros((n, 16, 128), F32)
    low, high = tail[:, 0:16], tail[:, 16:32]
    last = jnp.where(lane < 48, pltpu.roll(low, 48, 2), jnp.where(lane < 80, pltpu.roll(high, 96, 2), zero))
    return jnp.concatenate([jnp.where(lane < 80, low, zero), jnp.where(lane < 80, high, zero), last], axis=1)


def main_kernel(
    pulled, counts, tok_hbm, route_hbm, weights_hbm, cot_hbm,
    act_out, dx_out, grad_out,
    weights, cot, packed1, packed2,
    sa1, sb1, ma1, mb1, land1, sa2, sb2, ma2, mb2, land2, full,
    ba1, bb1, na1, nb1, back1, ba2, bb2, na2, nb2, back2,
    own_tok, pair_tok, ring, xk, xt, scale, cotp, hid, sig, pick,
    terms, got, zsend, zrecv, half,
    p1a, p1b, p2, pl_, q1a, q1b, q2, ql_, r1a, r1b, r2, rl_, t1a, t1b, t2, tl_,
    ps, rg, xs, ins,
):
    g, s = lax.axis_index("group"), lax.axis_index("shard")
    zh, y, c = g // 16, lax.rem(g // 2, NY), lax.rem(g, 2)
    zl, x = s // NX, lax.rem(s, NX)

    def gdev(zh_, y_, c_):
        return ((zh_ * NY + y_) * 2 + c_, s)

    def sdev(zl_, x_):
        return (g, zl_ * NX + x_)

    loads = [
        pltpu.make_async_copy(weights_hbm, weights, ins.at[0]),
        pltpu.make_async_copy(tok_hbm, own_tok.at[:, 0:D], ins.at[1]),
        pltpu.make_async_copy(route_hbm, own_tok.at[:, D:], ins.at[2]),
        pltpu.make_async_copy(cot_hbm, cot, ins.at[3]),
    ]
    for load in loads:
        load.start()

    bar = pltpu.get_barrier_semaphore()

    def greet(dev):
        pl.semaphore_signal(bar, inc=1, device_id=dev, device_id_type=MESH)

    for dy in range(1, NY):
        greet(gdev(zh, lax.rem(y + dy, NY), c))
        greet(gdev(zh, lax.rem(y + dy, NY), 1 - c))
    for dz in range(1, NZ):
        greet(gdev(lax.rem(zh + dz, NZ), y, c))
        greet(gdev(lax.rem(zh + dz, NZ), y, 1 - c))
    greet(gdev(zh, y, 1 - c))
    for dx in range(1, NX):
        greet(sdev(zl, lax.rem(x + dx, NX)))
    greet(sdev(1 - zl, x))

    loads[0].wait()

    def pack_one(e, carry):
        packed1[e] = jnp.concatenate([weights[e, :, 0:128], weights[e, :, 128:256]], axis=0)
        tail = jnp.concatenate([weights[e, :, 256:].astype(F32), jnp.zeros((ROWS, 384 - COLS), F32)], axis=1)
        packed2[e] = pack_tail(tail[None])[0].astype(BF)
        return carry

    lax.fori_loop(0, weights.shape[0], pack_one, 0)

    def fill(k, carry):
        zt, yt = k // NY, lax.rem(k, NY)
        sa1[yt, zt] = packed1[pulled[2 * k]]
        sb1[zt, yt] = packed1[pulled[2 * k + 1]]
        sa2[yt, zt] = packed2[pulled[2 * k]]
        sb2[zt, yt] = packed2[pulled[2 * k + 1]]
        return carry

    lax.fori_loop(0, NZ * NY, fill, 0)
    loads[1].wait()
    loads[2].wait()

    pl.semaphore_wait(bar, 29)

    def exchange(src_a, src_b, ia, ib, dst, s1a, s1b, s2, sl):
        def a1(dy):
            yt = lax.rem(y + dy, NY)
            return pltpu.make_async_remote_copy(
                src_a.at[yt], ia.at[y], s1a.at[0, dy], s1a.at[1, dy], device_id=gdev(zh, yt, c), device_id_type=MESH)

        def b1(dz):
            zt = lax.rem(zh + dz, NZ)
            return pltpu.make_async_remote_copy(
                src_b.at[zt], ib.at[zh], s1b.at[0, dz], s1b.at[1, dz], device_id=gdev(zt, y, c), device_id_type=MESH)

        def a2(dz, cross):
            zt = lax.rem(zh + dz, NZ)
            k = dz * 2 + cross
            return pltpu.make_async_remote_copy(
                ia.at[:, zt], dst.at[zh, :, c], s2.at[0, k], s2.at[1, k], device_id=gdev(zt, y, 0), device_id_type=MESH)

        def b2(dy, cross):
            yt = lax.rem(y + dy, NY)
            k = dy * 2 + cross
            return pltpu.make_async_remote_copy(
                ib.at[:, yt], dst.at[:, y, c], s2.at[0, k], s2.at[1, k], device_id=gdev(zh, yt, 1), device_id_type=MESH)

        la = pltpu.make_async_copy(src_a.at[y], ia.at[y], sl.at[0])
        lb = pltpu.make_async_copy(src_b.at[zh], ib.at[zh], sl.at[1])
        l2a = pltpu.make_async_copy(ia.at[:, zh], dst.at[zh, :, 0], sl.at[2])
        l2b = pltpu.make_async_copy(ib.at[:, y], dst.at[:, y, 1], sl.at[2])

        def start1():
            la.start()
            lb.start()
            for i, dy in enumerate(ORDER_Y):
                a1(dy).start()
                if i % 2 == 0 and i // 2 < 3:
                    b1(ORDER_Z[i // 2]).start()

        def turn_a():
            la.wait()
            for dy in ORDER_Y:
                a1(dy).wait()

            @pl.when(c == 0)
            def _():
                l2a.start()
                for dz in ORDER_Z:
                    a2(dz, 0).start()

            @pl.when(c == 1)
            def _():
                for dz in ORDER_Z + (0,):
                    a2(dz, 1).start()

        def turn_b():
            lb.wait()
            for dz in ORDER_Z:
                b1(dz).wait()

            @pl.when(c == 1)
            def _():
                l2b.start()
                for dy in ORDER_Y:
                    b2(dy, 0).start()

            @pl.when(c == 0)
            def _():
                for dy in ORDER_Y + (0,):
                    b2(dy, 1).start()

        def finish():
            @pl.when(c == 0)
            def _():
                l2a.wait()
                for dz in ORDER_Z:
                    a2(dz, 0).wait()
                for dz in ORDER_Z + (0,):
                    a2(dz, 1).wait_recv()
                for dy in ORDER_Y + (0,):
                    b2(dy, 1).wait_send()

            @pl.when(c == 1)
            def _():
                l2b.wait()
                for dy in ORDER_Y:
                    b2(dy, 0).wait()
                for dy in ORDER_Y + (0,):
                    b2(dy, 1).wait_recv()
                for dz in ORDER_Z + (0,):
                    a2(dz, 1).wait_send()

        return start1, turn_a, turn_b, finish

    pair = pltpu.make_async_remote_copy(
        own_tok, pair_tok, ps.at[0], ps.at[1], device_id=sdev(1 - zl, x), device_id_type=MESH)
    pair.start()
    w1 = exchange(sa1, sb1, ma1, mb1, land1, p1a, p1b, p2, pl_)
    w2 = exchange(sa2, sb2, ma2, mb2, land2, q1a, q1b, q2, ql_)
    w1[0]()
    w2[0]()

    pair.wait()
    mine, other = own_tok[...].astype(F32), pair_tok[...].astype(F32)
    ring[x] = jnp.concatenate(
        [jnp.where(zl == 0, mine, other), jnp.where(zl == 0, other, mine)], axis=0).astype(BF)

    right, left = lax.rem(x + 1, NX), lax.rem(x + NX - 1, NX)
    cut = 13 * 128

    def hop(step):
        a, b = lax.rem(x - step + 1 + NX, NX), lax.rem(x + step - 1, NX)
        if step < 4:
            ra, rb = ring.at[a], ring.at[b]
        else:
            ra, rb = ring.at[a, :, 0:cut], ring.at[b, :, cut:]
        k = 2 * (step - 1)
        return (
            pltpu.make_async_remote_copy(
                ra, ra, rg.at[0, k], rg.at[1, k], device_id=sdev(zl, right), device_id_type=MESH),
            pltpu.make_async_remote_copy(
                rb, rb, rg.at[0, k + 1], rg.at[1, k + 1], device_id=sdev(zl, left), device_id_type=MESH),
        )

    def hop_start(step):
        for copy in hop(step):
            copy.start()

    def hop_wait(step):
        for copy in hop(step):
            copy.wait()

    hop_start(1)
    loads[3].wait()
    cotp[:, 256:] = jnp.zeros((CAP, 128), F32)
    cotp[:, 0:COLS] = cot[...].astype(F32)

    column = lax.broadcasted_iota(jnp.int32, (1, 1024), 1)
    expert = jnp.zeros((1, 1024), jnp.int32)
    for k in range(NZ * NY * NC):
        expert = jnp.where(column // 16 == k, pulled[k], expert)
    for e in range(16):
        row = lax.broadcasted_iota(jnp.int32, (16, 1024), 0)
        hit = (row == lax.rem(column, 16)) & (expert == e)
        pick[16 * e:16 * e + 16] = jnp.where(hit, jnp.float32(1), jnp.float32(0)).astype(BF)

    hop_wait(1)
    hop_start(2)
    hop_wait(2)
    hop_start(3)
    w1[1]()
    w1[2]()
    hop_wait(3)
    hop_start(4)
    w2[1]()
    w2[2]()
    hop_wait(4)

    def gather_rows(lanes):
        parts = [ring[i, :, lanes].astype(F32) for i in range(NX)]
        return jnp.concatenate([p[0:TOK] for p in parts] + [p[TOK:] for p in parts], axis=0)

    def order(k, carry):
        rows = gather_rows(pl.ds(pl.multiple_of(k * KW, 128), KW))
        xk[k] = rows.astype(BF)
        xt[k] = rows.T.astype(BF)
        return carry

    lax.fori_loop(0, KC, order, 0)
    live = lax.broadcasted_iota(jnp.int32, (CAP, 128), 0) < counts[0]
    scale[...] = jnp.where(live, gather_rows(pl.ds(D, 128)), jnp.zeros((CAP, 128), F32))
    hid[...] = jnp.zeros((CAP, 384), F32)

    def activate(t):
        lanes = slice(128 * t, 128 * t + 128)
        h, sc = hid[:, lanes], scale[...]
        sigma = jax.nn.sigmoid(h)
        value = (sc * (h * sigma)).astype(BF)
        if t < 2:
            act_out[:, lanes] = value
        else:
            act_out[:, 256:COLS] = value[:, 0:80]
        sig[:, lanes] = (cotp[:, lanes] * sc * (sigma * (1.0 + h * (1.0 - sigma)))).astype(BF)

    w1[3]()

    def forward1(k, carry):
        blocks = land1[k // 2, pl.ds(lax.rem(k, 2) * 4, 4)].reshape(8, 96, 128)
        chunk = jnp.concatenate(
            [blocks[:, 0:ROWS].reshape(KW, 128), blocks[:, ROWS:].reshape(KW, 128)], axis=1)
        full[k, :, 0:256] = chunk
        hid[:, 0:256] += jnp.dot(xk[k], chunk, preferred_element_type=F32)
        return carry

    lax.fori_loop(0, KC, forward1, 0)
    activate(0)
    activate(1)

    def grads1(k, carry):
        part = jnp.dot(xt[k], sig[:, 0:256], preferred_element_type=F32).astype(BF)
        low, high = part[:, 0:128].reshape(8, ROWS, 128), part[:, 128:].reshape(8, ROWS, 128)
        zt, y0 = k // 2, lax.rem(k, 2) * 4
        for j in range(4):
            ba1[y0 + j, zt, 0:ROWS] = low[2 * j]
            ba1[y0 + j, zt, ROWS:] = high[2 * j]
            bb1[zt, y0 + j, 0:ROWS] = low[2 * j + 1]
            bb1[zt, y0 + j, ROWS:] = high[2 * j + 1]
        return carry

    lax.fori_loop(0, KC, grads1, 0)
    g1 = exchange(ba1, bb1, na1, nb1, back1, r1a, r1b, r2, rl_)
    g1[0]()

    w2[3]()

    def forward2(k, carry):
        blocks = land2[k // 2, pl.ds(lax.rem(k, 2) * 4, 4)].reshape(8, 32, 128)
        chunk = unpack_tail(blocks.astype(F32)).reshape(KW, 128).astype(BF)
        full[k, :, 256:] = chunk
        hid[:, 256:] += jnp.dot(xk[k], chunk, preferred_element_type=F32)
        return carry

    lax.fori_loop(0, KC, forward2, 0)
    activate(2)

    def grads2(k, carry):
        part = jnp.dot(xt[k], sig[:, 256:], preferred_element_type=F32)
        blocks = pack_tail(part.reshape(8, ROWS, 128)).astype(BF)
        zt, y0 = k // 2, lax.rem(k, 2) * 4
        for j in range(4):
            ba2[y0 + j, zt] = blocks[2 * j]
            bb2[zt, y0 + j] = blocks[2 * j + 1]
        return carry

    lax.fori_loop(0, KC, grads2, 0)
    g2 = exchange(ba2, bb2, na2, nb2, back2, t1a, t1b, t2, tl_)
    g2[0]()

    def inputs(k, carry):
        term = lax.dot_general(sig[...], full[k], (((1,), (1,)), ((), ())), preferred_element_type=F32)
        lanes = pl.ds(pl.multiple_of(k * KW, 128), KW)
        for i in range(NX):
            terms[i, :, lanes] = jnp.concatenate(
                [term[TOK * i:TOK * i + TOK], term[160 + TOK * i:160 + TOK * i + TOK]], axis=0).astype(BF)
        return carry

    lax.fori_loop(0, KC, inputs, 0)
    wide = D // 2

    def target(way, step):
        return lax.rem(x + 5 - step, NX) if way == 0 else lax.rem(x + NX - 5 + step, NX)

    def shift(way, step, part):
        lanes = slice(wide * part, wide * part + wide)
        return pltpu.make_async_remote_copy(
            terms.at[target(way, step), :, lanes], got.at[way, step - 1, :, lanes],
            xs.at[0, way, step - 1, part], xs.at[1, way, step - 1, part],
            device_id=sdev(zl, right if way == 0 else left), device_id_type=MESH)

    def pass_on(way, step, part):
        shift(way, step - 1, part).wait()
        to = target(way, step)

        def add(k, carry):
            lanes = pl.ds(pl.multiple_of(wide * part + k * KW, 128), KW)
            terms[to, :, lanes] = (
                terms[to, :, lanes].astype(F32) + got[way, step - 2, :, lanes].astype(F32)).astype(BF)
            return carry

        lax.fori_loop(0, wide // KW, add, 0)
        shift(way, step, part).start()

    shift(0, 1, 0).start()
    shift(1, 1, 1).start()
    shift(0, 2, 1).start()
    shift(1, 2, 0).start()
    pass_on(0, 2, 0)
    pass_on(1, 2, 1)
    for way, part in ((0, 1), (1, 0), (0, 0), (1, 1)):
        pass_on(way, 3, part)
    g1[1]()
    g1[2]()
    for way, part in ((0, 1), (1, 0), (0, 0), (1, 1)):
        pass_on(way, 4, part)
    g2[1]()
    g2[2]()
    for way, part in ((0, 1), (1, 0), (0, 0), (1, 1)):
        shift(way, 4, part).wait()

    def add_up(k, carry):
        lanes = pl.ds(pl.multiple_of(k * KW, 128), KW)
        total = terms[x, :, lanes].astype(F32) + got[0, 3, :, lanes].astype(F32) + got[1, 3, :, lanes].astype(F32)
        low, high = total[0:TOK], total[TOK:]
        half[:, lanes] = jnp.where(zl == 0, low, high)
        zsend[:, lanes] = jnp.where(zl == 0, high, low).astype(BF)
        return carry

    lax.fori_loop(0, KC, add_up, 0)
    last = pltpu.make_async_remote_copy(
        zsend, zrecv, ps.at[2], ps.at[3], device_id=sdev(1 - zl, x), device_id_type=MESH)
    last.start()

    def expert_sums(blocks):
        rows = [blocks[:, :, :, 16 * q:16 * q + 16].reshape(1024, 128) for q in range(2)]
        total = jnp.dot(pick[...], jnp.concatenate(rows, axis=1), preferred_element_type=F32)
        return total[:, 0:128].reshape(16, 16, 128), total[:, 128:].reshape(16, 16, 128)

    g1[3]()
    for pair_of in range(3):
        sums = expert_sums(back1[:, :, :, 32 * pair_of:32 * pair_of + 32])
        for i in range(2):
            q = 2 * pair_of + i
            grad_out[:, 16 * (q % 3):16 * (q % 3) + 16, 128 * (q // 3):128 * (q // 3) + 128] = sums[i]
    last.wait()
    dx_out[...] = (half[...] + zrecv[...].astype(F32)).astype(BF)
    g2[3]()
    low, high = expert_sums(back2[...])
    grad_out[:, :, 256:] = unpack_tail(jnp.concatenate([low, high], axis=1))[:, :, 0:80]


def shards(tokens, route_weight, counts, pulled, weights, cotangent):
    vmem, smem = pl.BlockSpec(memory_space=pltpu.VMEM), pl.BlockSpec(memory_space=pltpu.SMEM)
    dma = pltpu.SemaphoreType.DMA
    route = jnp.broadcast_to(route_weight[:, None], (TOK, 128))
    hbm = pl.BlockSpec(memory_space=pltpu.HBM)

    def blocks_of(n):
        outer = [(NY, NZ), (NZ, NY), (NY, NZ), (NZ, NY), (NZ, NY, NC)]
        return [pltpu.VMEM(shape + (n, 128), BF) for shape in outer]

    sems = [dma((2, NY)), dma((2, NZ)), dma((2, 2 * NY)), dma((3,))]
    return pl.pallas_call(
        main_kernel,
        out_shape=[
            jax.ShapeDtypeStruct((CAP, COLS), BF),
            jax.ShapeDtypeStruct((TOK, D), BF),
            jax.ShapeDtypeStruct(weights.shape, F32),
        ],
        in_specs=[smem, smem, hbm, hbm, hbm, hbm],
        out_specs=[vmem, vmem, vmem],
        scratch_shapes=[
            pltpu.VMEM((16, ROWS, COLS), BF),
            pltpu.VMEM((CAP, COLS), BF),
            pltpu.VMEM((16, 96, 128), BF),
            pltpu.VMEM((16, 32, 128), BF),
            *blocks_of(96),
            *blocks_of(32),
            pltpu.VMEM((KC, KW, 384), BF),
            *blocks_of(96),
            *blocks_of(32),
            pltpu.VMEM((TOK, D + 128), BF),
            pltpu.VMEM((TOK, D + 128), BF),
            pltpu.VMEM((NX, 2 * TOK, D + 128), BF),
            pltpu.VMEM((KC, CAP, KW), BF),
            pltpu.VMEM((KC, KW, CAP), BF),
            pltpu.VMEM((CAP, 128), F32),
            pltpu.VMEM((CAP, 384), F32),
            pltpu.VMEM((CAP, 384), F32),
            pltpu.VMEM((CAP, 384), BF),
            pltpu.VMEM((256, 1024), BF),
            pltpu.VMEM((NX, 2 * TOK, D), BF),
            pltpu.VMEM((2, 4, 2 * TOK, D), BF),
            pltpu.VMEM((TOK, D), BF),
            pltpu.VMEM((TOK, D), BF),
            pltpu.VMEM((TOK, D), F32),
            *sems, *sems, *sems, *sems,
            dma((4,)), dma((2, 8)), dma((2, 2, 4, 2)), dma((4,)),
        ],
        compiler_params=pltpu.CompilerParams(
            collective_id=1, has_side_effects=True, vmem_limit_bytes=36 << 20),
        name="exchange_and_compute",
    )(pulled, counts, tokens, route, weights, cotangent)


def solution(mesh):
    in_specs = (
        P(("group", "shard"), None),
        P(("group", "shard")),
        P("group"),
        P(),
        P(None, "group", "shard"),
        P("group", "shard"),
    )
    out_specs = (P("group", "shard"), P(("group", "shard"), None), P(None, "group", "shard"))
    return jax.shard_map(shards, mesh=mesh, in_specs=in_specs, out_specs=out_specs, check_vma=False)
```

```python
import functools

import jax
import jax.numpy as jnp
from jax import lax
from jax.experimental import pallas as pl
from jax.experimental.pallas import tpu as pltpu
from jax.sharding import PartitionSpec as P

MESH = pl.DeviceIdType.MESH
NZ, NY, NC, NX = 4, 8, 2, 8
ROWS, COLS, TOK = 48, 336, 20
CAP, D = 320, 3072
KC = 8
KW = D // KC
BF, F32 = jnp.bfloat16, jnp.float32
ORDER_Y = (4, 3, 5, 2, 6, 1, 7)
ORDER_Z = (2, 1, 3)


def pack_tail(tail):
    n = tail.shape[0]
    lane = lax.broadcasted_iota(jnp.int32, (n, 16, 128), 2)
    last = tail[:, 32:48]
    low = jnp.where(lane < 80, tail[:, 0:16], pltpu.roll(last, 80, 2))
    high = jnp.where(lane < 80, tail[:, 16:32], pltpu.roll(last, 32, 2))
    return jnp.concatenate([low, high], axis=1)


def unpack_tail(tail):
    n = tail.shape[0]
    lane = lax.broadcasted_iota(jnp.int32, (n, 16, 128), 2)
    zero = jnp.zeros((n, 16, 128), F32)
    low, high = tail[:, 0:16], tail[:, 16:32]
    last = jnp.where(lane < 48, pltpu.roll(low, 48, 2), jnp.where(lane < 80, pltpu.roll(high, 96, 2), zero))
    return jnp.concatenate([jnp.where(lane < 80, low, zero), jnp.where(lane < 80, high, zero), last], axis=1)


def main_kernel(
    pulled, counts, own_tok, weights, cot,
    act_out, dx_out, grad_out,
    packed1, packed2,
    sa1, sb1, ma1, mb1, land1, sa2, sb2, ma2, mb2, land2, full,
    ba1, bb1, na1, nb1, back1, ba2, bb2, na2, nb2, back2,
    pair_tok, ring, xk, xt, scale, cotp, hid, sig, pick,
    terms, got, zsend, zrecv, half,
    p1a, p1b, p2, pl_, q1a, q1b, q2, ql_, r1a, r1b, r2, rl_, t1a, t1b, t2, tl_,
    ps, rg, xs,
):
    g, s = lax.axis_index("group"), lax.axis_index("shard")
    zh, y, c = g // 16, lax.rem(g // 2, NY), lax.rem(g, 2)
    zl, x = s // NX, lax.rem(s, NX)

    def gdev(zh_, y_, c_):
        return ((zh_ * NY + y_) * 2 + c_, s)

    def sdev(zl_, x_):
        return (g, zl_ * NX + x_)

    bar = pltpu.get_barrier_semaphore()

    def greet(dev):
        pl.semaphore_signal(bar, inc=1, device_id=dev, device_id_type=MESH)

    for dy in range(1, NY):
        greet(gdev(zh, lax.rem(y + dy, NY), c))
        greet(gdev(zh, lax.rem(y + dy, NY), 1 - c))
    for dz in range(1, NZ):
        greet(gdev(lax.rem(zh + dz, NZ), y, c))
        greet(gdev(lax.rem(zh + dz, NZ), y, 1 - c))
    greet(gdev(zh, y, 1 - c))
    for dx in range(1, NX):
        greet(sdev(zl, lax.rem(x + dx, NX)))
    greet(sdev(1 - zl, x))

    def pack_one(e, carry):
        packed1[e] = jnp.concatenate([weights[e, :, 0:128], weights[e, :, 128:256]], axis=0)
        tail = jnp.concatenate([weights[e, :, 256:].astype(F32), jnp.zeros((ROWS, 384 - COLS), F32)], axis=1)
        packed2[e] = pack_tail(tail[None])[0].astype(BF)
        return carry

    lax.fori_loop(0, weights.shape[0], pack_one, 0)

    def fill(k, carry):
        zt, yt = k // NY, lax.rem(k, NY)
        sa1[yt, zt] = packed1[pulled[2 * k]]
        sb1[zt, yt] = packed1[pulled[2 * k + 1]]
        sa2[yt, zt] = packed2[pulled[2 * k]]
        sb2[zt, yt] = packed2[pulled[2 * k + 1]]
        return carry

    lax.fori_loop(0, NZ * NY, fill, 0)

    pl.semaphore_wait(bar, 29)

    def exchange(src_a, src_b, ia, ib, dst, s1a, s1b, s2, sl):
        def a1(dy):
            yt = lax.rem(y + dy, NY)
            return pltpu.make_async_remote_copy(
                src_a.at[yt], ia.at[y], s1a.at[0, dy], s1a.at[1, dy], device_id=gdev(zh, yt, c), device_id_type=MESH)

        def b1(dz):
            zt = lax.rem(zh + dz, NZ)
            return pltpu.make_async_remote_copy(
                src_b.at[zt], ib.at[zh], s1b.at[0, dz], s1b.at[1, dz], device_id=gdev(zt, y, c), device_id_type=MESH)

        def a2(dz, cross):
            zt = lax.rem(zh + dz, NZ)
            k = dz * 2 + cross
            return pltpu.make_async_remote_copy(
                ia.at[:, zt], dst.at[zh, :, c], s2.at[0, k], s2.at[1, k], device_id=gdev(zt, y, 0), device_id_type=MESH)

        def b2(dy, cross):
            yt = lax.rem(y + dy, NY)
            k = dy * 2 + cross
            return pltpu.make_async_remote_copy(
                ib.at[:, yt], dst.at[:, y, c], s2.at[0, k], s2.at[1, k], device_id=gdev(zh, yt, 1), device_id_type=MESH)

        la = pltpu.make_async_copy(src_a.at[y], ia.at[y], sl.at[0])
        lb = pltpu.make_async_copy(src_b.at[zh], ib.at[zh], sl.at[1])
        l2a = pltpu.make_async_copy(ia.at[:, zh], dst.at[zh, :, 0], sl.at[2])
        l2b = pltpu.make_async_copy(ib.at[:, y], dst.at[:, y, 1], sl.at[2])

        def start_b(dz):
            b1(dz).start()

        def start_a():
            la.start()
            lb.start()
            for dy in ORDER_Y:
                a1(dy).start()

        def start1():
            for dz in ORDER_Z:
                start_b(dz)
            start_a()

        def turn_a():
            la.wait()
            for dy in ORDER_Y:
                a1(dy).wait()

            @pl.when(c == 0)
            def _():
                l2a.start()
                for dz in ORDER_Z:
                    a2(dz, 0).start()

            @pl.when(c == 1)
            def _():
                for dz in ORDER_Z + (0,):
                    a2(dz, 1).start()

        def turn_b():
            lb.wait()
            for dz in ORDER_Z:
                b1(dz).wait()

            @pl.when(c == 1)
            def _():
                l2b.start()
                for dy in ORDER_Y:
                    b2(dy, 0).start()

            @pl.when(c == 0)
            def _():
                for dy in ORDER_Y + (0,):
                    b2(dy, 1).start()

        def finish():
            @pl.when(c == 0)
            def _():
                l2a.wait()
                for dz in ORDER_Z:
                    a2(dz, 0).wait()
                for dz in ORDER_Z + (0,):
                    a2(dz, 1).wait_recv()
                for dy in ORDER_Y + (0,):
                    b2(dy, 1).wait_send()

            @pl.when(c == 1)
            def _():
                l2b.wait()
                for dy in ORDER_Y:
                    b2(dy, 0).wait()
                for dy in ORDER_Y + (0,):
                    b2(dy, 1).wait_recv()
                for dz in ORDER_Z + (0,):
                    a2(dz, 1).wait_send()

        return start1, turn_a, turn_b, finish, start_a, start_b

    pair = pltpu.make_async_remote_copy(
        own_tok, pair_tok, ps.at[0], ps.at[1], device_id=sdev(1 - zl, x), device_id_type=MESH)
    pair.start()
    w1 = exchange(sa1, sb1, ma1, mb1, land1, p1a, p1b, p2, pl_)
    w2 = exchange(sa2, sb2, ma2, mb2, land2, q1a, q1b, q2, ql_)
    w1[0]()
    w2[0]()

    pair.wait()
    mine, other = own_tok[...].astype(F32), pair_tok[...].astype(F32)
    ring[x] = jnp.concatenate(
        [jnp.where(zl == 0, mine, other), jnp.where(zl == 0, other, mine)], axis=0).astype(BF)

    right, left = lax.rem(x + 1, NX), lax.rem(x + NX - 1, NX)
    cut = 13 * 128

    def hop(step):
        a, b = lax.rem(x - step + 1 + NX, NX), lax.rem(x + step - 1, NX)
        if step < 4:
            ra, rb = ring.at[a], ring.at[b]
        else:
            ra, rb = ring.at[a, :, 0:cut], ring.at[b, :, cut:]
        k = 2 * (step - 1)
        return (
            pltpu.make_async_remote_copy(
                ra, ra, rg.at[0, k], rg.at[1, k], device_id=sdev(zl, right), device_id_type=MESH),
            pltpu.make_async_remote_copy(
                rb, rb, rg.at[0, k + 1], rg.at[1, k + 1], device_id=sdev(zl, left), device_id_type=MESH),
        )

    def hop_start(step):
        for copy in hop(step):
            copy.start()

    def hop_wait(step):
        for copy in hop(step):
            copy.wait()

    hop_start(1)
    cotp[:, 256:] = jnp.zeros((CAP, 128), F32)
    cotp[:, 0:COLS] = cot[...].astype(F32)

    column = lax.broadcasted_iota(jnp.int32, (1, 1024), 1)
    expert = jnp.zeros((1, 1024), jnp.int32)
    for k in range(NZ * NY * NC):
        expert = jnp.where(column // 16 == k, pulled[k], expert)
    for e in range(16):
        row = lax.broadcasted_iota(jnp.int32, (16, 1024), 0)
        hit = (row == lax.rem(column, 16)) & (expert == e)
        pick[16 * e:16 * e + 16] = jnp.where(hit, jnp.float32(1), jnp.float32(0)).astype(BF)

    hop_wait(1)
    hop_start(2)
    hop_wait(2)
    hop_start(3)
    w1[1]()
    w1[2]()
    hop_wait(3)
    hop_start(4)
    w2[1]()
    w2[2]()
    hop_wait(4)

    def gather_rows(lanes):
        parts = [ring[i, :, lanes].astype(F32) for i in range(NX)]
        return jnp.concatenate([p[0:TOK] for p in parts] + [p[TOK:] for p in parts], axis=0)

    def order(k, carry):
        rows = gather_rows(pl.ds(pl.multiple_of(k * KW, 128), KW))
        xk[k] = rows.astype(BF)
        xt[k] = rows.T.astype(BF)
        return carry

    lax.fori_loop(0, KC, order, 0)
    live = lax.broadcasted_iota(jnp.int32, (CAP, 128), 0) < counts[0]
    scale[...] = jnp.where(live, gather_rows(pl.ds(D, 128)), jnp.zeros((CAP, 128), F32))
    hid[...] = jnp.zeros((CAP, 384), F32)

    def activate(t):
        lanes = slice(128 * t, 128 * t + 128)
        h, sc = hid[:, lanes], scale[...]
        sigma = jax.nn.sigmoid(h)
        value = (sc * (h * sigma)).astype(BF)
        if t < 2:
            act_out[:, lanes] = value
        else:
            act_out[:, 256:COLS] = value[:, 0:80]
        sig[:, lanes] = (cotp[:, lanes] * sc * (sigma * (1.0 + h * (1.0 - sigma)))).astype(BF)

    w1[3]()

    def forward1(k, carry):
        blocks = land1[k // 2, pl.ds(lax.rem(k, 2) * 4, 4)].reshape(8, 96, 128)
        chunk = jnp.concatenate(
            [blocks[:, 0:ROWS].reshape(KW, 128), blocks[:, ROWS:].reshape(KW, 128)], axis=1)
        full[k, :, 0:256] = chunk
        hid[:, 0:256] += jnp.dot(xk[k], chunk, preferred_element_type=F32)
        return carry

    lax.fori_loop(0, KC, forward1, 0)
    activate(0)
    activate(1)

    def grads1(k, carry):
        part = jnp.dot(xt[k], sig[:, 0:256], preferred_element_type=F32).astype(BF)
        low, high = part[:, 0:128].reshape(8, ROWS, 128), part[:, 128:].reshape(8, ROWS, 128)
        zt, y0 = k // 2, lax.rem(k, 2) * 4
        for j in range(4):
            ba1[y0 + j, zt, 0:ROWS] = low[2 * j]
            ba1[y0 + j, zt, ROWS:] = high[2 * j]
            bb1[zt, y0 + j, 0:ROWS] = low[2 * j + 1]
            bb1[zt, y0 + j, ROWS:] = high[2 * j + 1]
        return carry

    g1 = exchange(ba1, bb1, na1, nb1, back1, r1a, r1b, r2, rl_)
    for dz in ORDER_Z + (0,):
        zt_ = lax.rem(zh + dz, NZ)
        lax.fori_loop(0, 2, lambda i, carry: grads1(2 * zt_ + i, carry), 0)
        if dz:
            g1[5](dz)
    g1[4]()

    w2[3]()

    def forward2(k, carry):
        blocks = land2[k // 2, pl.ds(lax.rem(k, 2) * 4, 4)].reshape(8, 32, 128)
        chunk = unpack_tail(blocks.astype(F32)).reshape(KW, 128).astype(BF)
        full[k, :, 256:] = chunk
        hid[:, 256:] += jnp.dot(xk[k], chunk, preferred_element_type=F32)
        return carry

    lax.fori_loop(0, KC, forward2, 0)
    activate(2)

    def grads2(k, carry):
        part = jnp.dot(xt[k], sig[:, 256:], preferred_element_type=F32)
        blocks = pack_tail(part.reshape(8, ROWS, 128)).astype(BF)
        zt, y0 = k // 2, lax.rem(k, 2) * 4
        for j in range(4):
            ba2[y0 + j, zt] = blocks[2 * j]
            bb2[zt, y0 + j] = blocks[2 * j + 1]
        return carry

    lax.fori_loop(0, KC, grads2, 0)
    g2 = exchange(ba2, bb2, na2, nb2, back2, t1a, t1b, t2, tl_)
    g2[0]()

    def inputs(k, carry):
        term = lax.dot_general(sig[...], full[k], (((1,), (1,)), ((), ())), preferred_element_type=F32)
        lanes = pl.ds(pl.multiple_of(k * KW, 128), KW)
        for i in range(NX):
            terms[i, :, lanes] = jnp.concatenate(
                [term[TOK * i:TOK * i + TOK], term[160 + TOK * i:160 + TOK * i + TOK]], axis=0).astype(BF)
        return carry

    lax.fori_loop(0, KC, inputs, 0)
    wide = D // 2

    def target(way, step):
        return lax.rem(x + 5 - step, NX) if way == 0 else lax.rem(x + NX - 5 + step, NX)

    def shift(way, step, part):
        lanes = slice(wide * part, wide * part + wide)
        return pltpu.make_async_remote_copy(
            terms.at[target(way, step), :, lanes], got.at[way, step - 1, :, lanes],
            xs.at[0, way, step - 1, part], xs.at[1, way, step - 1, part],
            device_id=sdev(zl, right if way == 0 else left), device_id_type=MESH)

    def pass_on(way, step, part):
        shift(way, step - 1, part).wait()
        to = target(way, step)

        def add(k, carry):
            lanes = pl.ds(pl.multiple_of(wide * part + k * KW, 128), KW)
            terms[to, :, lanes] = (
                terms[to, :, lanes].astype(F32) + got[way, step - 2, :, lanes].astype(F32)).astype(BF)
            return carry

        lax.fori_loop(0, wide // KW, add, 0)
        shift(way, step, part).start()

    shift(0, 1, 0).start()
    shift(1, 1, 1).start()
    shift(0, 2, 1).start()
    shift(1, 2, 0).start()
    pass_on(0, 2, 0)
    pass_on(1, 2, 1)
    for way, part in ((0, 1), (1, 0), (0, 0), (1, 1)):
        pass_on(way, 3, part)
    g1[1]()
    g1[2]()
    for way, part in ((0, 1), (1, 0), (0, 0), (1, 1)):
        pass_on(way, 4, part)
    g2[1]()
    g2[2]()
    for way, part in ((0, 1), (1, 0), (0, 0), (1, 1)):
        shift(way, 4, part).wait()

    def add_up(k, carry):
        lanes = pl.ds(pl.multiple_of(k * KW, 128), KW)
        total = terms[x, :, lanes].astype(F32) + got[0, 3, :, lanes].astype(F32) + got[1, 3, :, lanes].astype(F32)
        low, high = total[0:TOK], total[TOK:]
        half[:, lanes] = jnp.where(zl == 0, low, high)
        zsend[:, lanes] = jnp.where(zl == 0, high, low).astype(BF)
        return carry

    lax.fori_loop(0, KC, add_up, 0)
    last = pltpu.make_async_remote_copy(
        zsend, zrecv, ps.at[2], ps.at[3], device_id=sdev(1 - zl, x), device_id_type=MESH)
    last.start()

    def expert_sums(blocks):
        rows = [blocks[:, :, :, 16 * q:16 * q + 16].reshape(1024, 128) for q in range(2)]
        total = jnp.dot(pick[...], jnp.concatenate(rows, axis=1), preferred_element_type=F32)
        return total[:, 0:128].reshape(16, 16, 128), total[:, 128:].reshape(16, 16, 128)

    g1[3]()
    for pair_of in range(3):
        sums = expert_sums(back1[:, :, :, 32 * pair_of:32 * pair_of + 32])
        for i in range(2):
            q = 2 * pair_of + i
            grad_out[:, 16 * (q % 3):16 * (q % 3) + 16, 128 * (q // 3):128 * (q // 3) + 128] = sums[i]
    last.wait()
    dx_out[...] = (half[...] + zrecv[...].astype(F32)).astype(BF)
    g2[3]()
    low, high = expert_sums(back2[...])
    grad_out[:, :, 256:] = unpack_tail(jnp.concatenate([low, high], axis=1))[:, :, 0:80]


def shards(tokens, route_weight, counts, pulled, weights, cotangent):
    vmem, smem = pl.BlockSpec(memory_space=pltpu.VMEM), pl.BlockSpec(memory_space=pltpu.SMEM)
    dma = pltpu.SemaphoreType.DMA
    lane = lax.broadcasted_iota(jnp.int32, (TOK, D + 128), 1)
    both = jnp.where(lane < D, jnp.pad(tokens, ((0, 0), (0, 128))), route_weight[:, None])
    def blocks_of(n):
        outer = [(NY, NZ), (NZ, NY), (NY, NZ), (NZ, NY), (NZ, NY, NC)]
        return [pltpu.VMEM(shape + (n, 128), BF) for shape in outer]

    sems = [dma((2, NY)), dma((2, NZ)), dma((2, 2 * NY)), dma((3,))]
    return pl.pallas_call(
        main_kernel,
        out_shape=[
            jax.ShapeDtypeStruct((CAP, COLS), BF),
            jax.ShapeDtypeStruct((TOK, D), BF),
            jax.ShapeDtypeStruct(weights.shape, F32),
        ],
        in_specs=[smem, smem, vmem, vmem, vmem],
        out_specs=[vmem, vmem, vmem],
        scratch_shapes=[
            pltpu.VMEM((16, 96, 128), BF),
            pltpu.VMEM((16, 32, 128), BF),
            *blocks_of(96),
            *blocks_of(32),
            pltpu.VMEM((KC, KW, 384), BF),
            *blocks_of(96),
            *blocks_of(32),
            pltpu.VMEM((TOK, D + 128), BF),
            pltpu.VMEM((NX, 2 * TOK, D + 128), BF),
            pltpu.VMEM((KC, CAP, KW), BF),
            pltpu.VMEM((KC, KW, CAP), BF),
            pltpu.VMEM((CAP, 128), F32),
            pltpu.VMEM((CAP, 384), F32),
            pltpu.VMEM((CAP, 384), F32),
            pltpu.VMEM((CAP, 384), BF),
            pltpu.VMEM((256, 1024), BF),
            pltpu.VMEM((NX, 2 * TOK, D), BF),
            pltpu.VMEM((2, 4, 2 * TOK, D), BF),
            pltpu.VMEM((TOK, D), BF),
            pltpu.VMEM((TOK, D), BF),
            pltpu.VMEM((TOK, D), F32),
            *sems, *sems, *sems, *sems,
            dma((4,)), dma((2, 8)), dma((2, 2, 4, 2)),
        ],
        compiler_params=pltpu.CompilerParams(
            collective_id=1, has_side_effects=True, vmem_limit_bytes=36 << 20),
        name="exchange_and_compute",
    )(pulled, counts, both, weights, cotangent)


def solution(mesh):
    in_specs = (
        P(("group", "shard"), None),
        P(("group", "shard")),
        P("group"),
        P(),
        P(None, "group", "shard"),
        P("group", "shard"),
    )
    out_specs = (P("group", "shard"), P(("group", "shard"), None), P(None, "group", "shard"))
    return jax.shard_map(shards, mesh=mesh, in_specs=in_specs, out_specs=out_specs, check_vma=False)
```

```python
import functools

import jax
import jax.numpy as jnp
from jax import lax
from jax.experimental import pallas as pl
from jax.experimental.pallas import tpu as pltpu
from jax.sharding import PartitionSpec as P

MESH = pl.DeviceIdType.MESH
NZ, NY, NC, NX = 4, 8, 2, 8
ROWS, COLS, TOK = 48, 336, 20
CAP, D = 320, 3072
KC = 8
KW = D // KC
BF, F32 = jnp.bfloat16, jnp.float32
ORDER_Y = (4, 3, 5, 2, 6, 1, 7)
ORDER_Z = (2, 1, 3)


def pack_tail(tail):
    n = tail.shape[0]
    lane = lax.broadcasted_iota(jnp.int32, (n, 16, 128), 2)
    last = tail[:, 32:48]
    low = jnp.where(lane < 80, tail[:, 0:16], pltpu.roll(last, 80, 2))
    high = jnp.where(lane < 80, tail[:, 16:32], pltpu.roll(last, 32, 2))
    return jnp.concatenate([low, high], axis=1)


def unpack_tail(tail):
    n = tail.shape[0]
    lane = lax.broadcasted_iota(jnp.int32, (n, 16, 128), 2)
    zero = jnp.zeros((n, 16, 128), F32)
    low, high = tail[:, 0:16], tail[:, 16:32]
    last = jnp.where(lane < 48, pltpu.roll(low, 48, 2), jnp.where(lane < 80, pltpu.roll(high, 96, 2), zero))
    return jnp.concatenate([jnp.where(lane < 80, low, zero), jnp.where(lane < 80, high, zero), last], axis=1)


def main_kernel(
    pulled, counts, own_tok, weights, cot,
    act_out, dx_out, grad_out,
    packed1, packed2,
    sa1, sb1, ma1, mb1, land1, sa2, sb2, ma2, mb2, land2, full,
    ba1, bb1, na1, nb1, back1, ba2, bb2, na2, nb2, back2,
    pair_tok, ring, xk, xt, scale, cotp, hid, sig, pick,
    terms, got, zsend, zrecv, half,
    p1a, p1b, p2, pl_, q1a, q1b, q2, ql_, r1a, r1b, r2, rl_, t1a, t1b, t2, tl_,
    ps, rg, xs,
):
    g, s = lax.axis_index("group"), lax.axis_index("shard")
    zh, y, c = g // 16, lax.rem(g // 2, NY), lax.rem(g, 2)
    zl, x = s // NX, lax.rem(s, NX)

    def gdev(zh_, y_, c_):
        return ((zh_ * NY + y_) * 2 + c_, s)

    def sdev(zl_, x_):
        return (g, zl_ * NX + x_)

    bar = pltpu.get_barrier_semaphore()

    def greet(dev):
        pl.semaphore_signal(bar, inc=1, device_id=dev, device_id_type=MESH)

    for dy in range(1, NY):
        greet(gdev(zh, lax.rem(y + dy, NY), c))
        greet(gdev(zh, lax.rem(y + dy, NY), 1 - c))
    for dz in range(1, NZ):
        greet(gdev(lax.rem(zh + dz, NZ), y, c))
        greet(gdev(lax.rem(zh + dz, NZ), y, 1 - c))
    greet(gdev(zh, y, 1 - c))
    for dx in range(1, NX):
        greet(sdev(zl, lax.rem(x + dx, NX)))
    greet(sdev(1 - zl, x))

    def pack_main(e, carry):
        packed1[e] = jnp.concatenate([weights[e, :, 0:128], weights[e, :, 128:256]], axis=0)
        return carry

    lax.fori_loop(0, weights.shape[0], pack_main, 0)
    pl.semaphore_wait(bar, 29)

    def exchange(src_a, src_b, ia, ib, dst, s1a, s1b, s2, sl):
        def a1(dy):
            yt = lax.rem(y + dy, NY)
            return pltpu.make_async_remote_copy(
                src_a.at[yt], ia.at[y], s1a.at[0, dy], s1a.at[1, dy], device_id=gdev(zh, yt, c), device_id_type=MESH)

        def b1(dz):
            zt = lax.rem(zh + dz, NZ)
            return pltpu.make_async_remote_copy(
                src_b.at[zt], ib.at[zh], s1b.at[0, dz], s1b.at[1, dz], device_id=gdev(zt, y, c), device_id_type=MESH)

        def a2(dz, cross):
            zt = lax.rem(zh + dz, NZ)
            k = dz * 2 + cross
            return pltpu.make_async_remote_copy(
                ia.at[:, zt], dst.at[zh, :, c], s2.at[0, k], s2.at[1, k], device_id=gdev(zt, y, 0), device_id_type=MESH)

        def b2(dy, cross):
            yt = lax.rem(y + dy, NY)
            k = dy * 2 + cross
            return pltpu.make_async_remote_copy(
                ib.at[:, yt], dst.at[:, y, c], s2.at[0, k], s2.at[1, k], device_id=gdev(zh, yt, 1), device_id_type=MESH)

        la = pltpu.make_async_copy(src_a.at[y], ia.at[y], sl.at[0])
        lb = pltpu.make_async_copy(src_b.at[zh], ib.at[zh], sl.at[1])
        l2a = pltpu.make_async_copy(ia.at[:, zh], dst.at[zh, :, 0], sl.at[2])
        l2b = pltpu.make_async_copy(ib.at[:, y], dst.at[:, y, 1], sl.at[2])

        def start_b(dz):
            b1(dz).start()

        def start_a():
            la.start()
            lb.start()
            for dy in ORDER_Y:
                a1(dy).start()

        def start1():
            for dz in ORDER_Z:
                start_b(dz)
            start_a()

        def turn_a():
            la.wait()
            for dy in ORDER_Y:
                a1(dy).wait()

            @pl.when(c == 0)
            def _():
                l2a.start()
                for dz in ORDER_Z:
                    a2(dz, 0).start()

            @pl.when(c == 1)
            def _():
                for dz in ORDER_Z + (0,):
                    a2(dz, 1).start()

        def turn_b():
            lb.wait()
            for dz in ORDER_Z:
                b1(dz).wait()

            @pl.when(c == 1)
            def _():
                l2b.start()
                for dy in ORDER_Y:
                    b2(dy, 0).start()

            @pl.when(c == 0)
            def _():
                for dy in ORDER_Y + (0,):
                    b2(dy, 1).start()

        def finish():
            @pl.when(c == 0)
            def _():
                l2a.wait()
                for dz in ORDER_Z:
                    a2(dz, 0).wait()
                for dz in ORDER_Z + (0,):
                    a2(dz, 1).wait_recv()
                for dy in ORDER_Y + (0,):
                    b2(dy, 1).wait_send()

            @pl.when(c == 1)
            def _():
                l2b.wait()
                for dy in ORDER_Y:
                    b2(dy, 0).wait()
                for dy in ORDER_Y + (0,):
                    b2(dy, 1).wait_recv()
                for dz in ORDER_Z + (0,):
                    a2(dz, 1).wait_send()

        return start1, turn_a, turn_b, finish, start_a, start_b

    pair = pltpu.make_async_remote_copy(
        own_tok, pair_tok, ps.at[0], ps.at[1], device_id=sdev(1 - zl, x), device_id_type=MESH)
    pair.start()
    w1 = exchange(sa1, sb1, ma1, mb1, land1, p1a, p1b, p2, pl_)
    w2 = exchange(sa2, sb2, ma2, mb2, land2, q1a, q1b, q2, ql_)

    def fill_b(zt, yt, carry):
        sb1[zt, yt] = packed1[pulled[2 * (zt * NY + yt) + 1]]
        return carry

    def fill_a(k, carry):
        sa1[lax.rem(k, NY), k // NY] = packed1[pulled[2 * k]]
        return carry

    for dz in ORDER_Z + (0,):
        lax.fori_loop(0, NY, functools.partial(fill_b, lax.rem(zh + dz, NZ)), 0)
        if dz:
            w1[5](dz)
    lax.fori_loop(0, NZ * NY, fill_a, 0)
    w1[4]()

    def pack_rest(e, carry):
        tail = jnp.concatenate([weights[e, :, 256:].astype(F32), jnp.zeros((ROWS, 384 - COLS), F32)], axis=1)
        packed2[e] = pack_tail(tail[None])[0].astype(BF)
        return carry

    def fill_rest(k, carry):
        zt, yt = k // NY, lax.rem(k, NY)
        sa2[yt, zt] = packed2[pulled[2 * k]]
        sb2[zt, yt] = packed2[pulled[2 * k + 1]]
        return carry

    lax.fori_loop(0, weights.shape[0], pack_rest, 0)
    lax.fori_loop(0, NZ * NY, fill_rest, 0)
    w2[0]()

    pair.wait()
    mine, other = own_tok[...].astype(F32), pair_tok[...].astype(F32)
    ring[x] = jnp.concatenate(
        [jnp.where(zl == 0, mine, other), jnp.where(zl == 0, other, mine)], axis=0).astype(BF)

    right, left = lax.rem(x + 1, NX), lax.rem(x + NX - 1, NX)
    cut = 13 * 128

    def hop(step):
        a, b = lax.rem(x - step + 1 + NX, NX), lax.rem(x + step - 1, NX)
        if step < 4:
            ra, rb = ring.at[a], ring.at[b]
        else:
            ra, rb = ring.at[a, :, 0:cut], ring.at[b, :, cut:]
        k = 2 * (step - 1)
        return (
            pltpu.make_async_remote_copy(
                ra, ra, rg.at[0, k], rg.at[1, k], device_id=sdev(zl, right), device_id_type=MESH),
            pltpu.make_async_remote_copy(
                rb, rb, rg.at[0, k + 1], rg.at[1, k + 1], device_id=sdev(zl, left), device_id_type=MESH),
        )

    def hop_start(step):
        for copy in hop(step):
            copy.start()

    def hop_wait(step):
        for copy in hop(step):
            copy.wait()

    hop_start(1)
    cotp[:, 256:] = jnp.zeros((CAP, 128), F32)
    cotp[:, 0:COLS] = cot[...].astype(F32)

    column = lax.broadcasted_iota(jnp.int32, (1, 1024), 1)
    expert = jnp.zeros((1, 1024), jnp.int32)
    for k in range(NZ * NY * NC):
        expert = jnp.where(column // 16 == k, pulled[k], expert)
    for e in range(16):
        row = lax.broadcasted_iota(jnp.int32, (16, 1024), 0)
        hit = (row == lax.rem(column, 16)) & (expert == e)
        pick[16 * e:16 * e + 16] = jnp.where(hit, jnp.float32(1), jnp.float32(0)).astype(BF)

    hop_wait(1)
    hop_start(2)
    hop_wait(2)
    hop_start(3)
    w1[1]()
    w1[2]()
    hop_wait(3)
    hop_start(4)
    w2[1]()
    w2[2]()
    hop_wait(4)

    def gather_rows(lanes):
        parts = [ring[i, :, lanes].astype(F32) for i in range(NX)]
        return jnp.concatenate([p[0:TOK] for p in parts] + [p[TOK:] for p in parts], axis=0)

    def order(k, carry):
        rows = gather_rows(pl.ds(pl.multiple_of(k * KW, 128), KW))
        xk[k] = rows.astype(BF)
        xt[k] = rows.T.astype(BF)
        return carry

    lax.fori_loop(0, KC, order, 0)
    live = lax.broadcasted_iota(jnp.int32, (CAP, 128), 0) < counts[0]
    scale[...] = jnp.where(live, gather_rows(pl.ds(D, 128)), jnp.zeros((CAP, 128), F32))
    hid[...] = jnp.zeros((CAP, 384), F32)

    def activate(t):
        lanes = slice(128 * t, 128 * t + 128)
        h, sc = hid[:, lanes], scale[...]
        sigma = jax.nn.sigmoid(h)
        value = (sc * (h * sigma)).astype(BF)
        if t < 2:
            act_out[:, lanes] = value
        else:
            act_out[:, 256:COLS] = value[:, 0:80]
        sig[:, lanes] = (cotp[:, lanes] * sc * (sigma * (1.0 + h * (1.0 - sigma)))).astype(BF)

    w1[3]()

    def forward1(k, carry):
        blocks = land1[k // 2, pl.ds(lax.rem(k, 2) * 4, 4)].reshape(8, 96, 128)
        chunk = jnp.concatenate(
            [blocks[:, 0:ROWS].reshape(KW, 128), blocks[:, ROWS:].reshape(KW, 128)], axis=1)
        full[k, :, 0:256] = chunk
        hid[:, 0:256] += jnp.dot(xk[k], chunk, preferred_element_type=F32)
        return carry

    lax.fori_loop(0, KC, forward1, 0)
    activate(0)
    activate(1)

    def grads1(k, carry):
        part = jnp.dot(xt[k], sig[:, 0:256], preferred_element_type=F32).astype(BF)
        low, high = part[:, 0:128].reshape(8, ROWS, 128), part[:, 128:].reshape(8, ROWS, 128)
        zt, y0 = k // 2, lax.rem(k, 2) * 4
        for j in range(4):
            ba1[y0 + j, zt, 0:ROWS] = low[2 * j]
            ba1[y0 + j, zt, ROWS:] = high[2 * j]
            bb1[zt, y0 + j, 0:ROWS] = low[2 * j + 1]
            bb1[zt, y0 + j, ROWS:] = high[2 * j + 1]
        return carry

    g1 = exchange(ba1, bb1, na1, nb1, back1, r1a, r1b, r2, rl_)
    for dz in ORDER_Z + (0,):
        zt_ = lax.rem(zh + dz, NZ)
        lax.fori_loop(0, 2, lambda i, carry: grads1(2 * zt_ + i, carry), 0)
        if dz:
            g1[5](dz)
    g1[4]()

    w2[3]()

    def forward2(k, carry):
        blocks = land2[k // 2, pl.ds(lax.rem(k, 2) * 4, 4)].reshape(8, 32, 128)
        chunk = unpack_tail(blocks.astype(F32)).reshape(KW, 128).astype(BF)
        full[k, :, 256:] = chunk
        hid[:, 256:] += jnp.dot(xk[k], chunk, preferred_element_type=F32)
        return carry

    lax.fori_loop(0, KC, forward2, 0)
    activate(2)

    def grads2(k, carry):
        part = jnp.dot(xt[k], sig[:, 256:], preferred_element_type=F32)
        blocks = pack_tail(part.reshape(8, ROWS, 128)).astype(BF)
        zt, y0 = k // 2, lax.rem(k, 2) * 4
        for j in range(4):
            ba2[y0 + j, zt] = blocks[2 * j]
            bb2[zt, y0 + j] = blocks[2 * j + 1]
        return carry

    lax.fori_loop(0, KC, grads2, 0)
    g2 = exchange(ba2, bb2, na2, nb2, back2, t1a, t1b, t2, tl_)
    g2[0]()

    def inputs(k, carry):
        term = lax.dot_general(sig[...], full[k], (((1,), (1,)), ((), ())), preferred_element_type=F32)
        lanes = pl.ds(pl.multiple_of(k * KW, 128), KW)
        for i in range(NX):
            terms[i, :, lanes] = jnp.concatenate(
                [term[TOK * i:TOK * i + TOK], term[160 + TOK * i:160 + TOK * i + TOK]], axis=0).astype(BF)
        return carry

    lax.fori_loop(0, KC, inputs, 0)
    wide = D // 2

    def target(way, step):
        return lax.rem(x + 5 - step, NX) if way == 0 else lax.rem(x + NX - 5 + step, NX)

    def shift(way, step, part):
        lanes = slice(wide * part, wide * part + wide)
        return pltpu.make_async_remote_copy(
            terms.at[target(way, step), :, lanes], got.at[way, step - 1, :, lanes],
            xs.at[0, way, step - 1, part], xs.at[1, way, step - 1, part],
            device_id=sdev(zl, right if way == 0 else left), device_id_type=MESH)

    def pass_on(way, step, part):
        shift(way, step - 1, part).wait()
        to = target(way, step)

        def add(k, carry):
            lanes = pl.ds(pl.multiple_of(wide * part + k * KW, 128), KW)
            terms[to, :, lanes] = (
                terms[to, :, lanes].astype(F32) + got[way, step - 2, :, lanes].astype(F32)).astype(BF)
            return carry

        lax.fori_loop(0, wide // KW, add, 0)
        shift(way, step, part).start()

    shift(0, 1, 0).start()
    shift(1, 1, 1).start()
    shift(0, 2, 1).start()
    shift(1, 2, 0).start()
    pass_on(0, 2, 0)
    pass_on(1, 2, 1)
    for way, part in ((0, 1), (1, 0), (0, 0), (1, 1)):
        pass_on(way, 3, part)
    g1[1]()
    g1[2]()
    for way, part in ((0, 1), (1, 0), (0, 0), (1, 1)):
        pass_on(way, 4, part)
    g2[1]()
    g2[2]()
    for way, part in ((0, 1), (1, 0), (0, 0), (1, 1)):
        shift(way, 4, part).wait()

    def add_up(k, carry):
        lanes = pl.ds(pl.multiple_of(k * KW, 128), KW)
        total = terms[x, :, lanes].astype(F32) + got[0, 3, :, lanes].astype(F32) + got[1, 3, :, lanes].astype(F32)
        low, high = total[0:TOK], total[TOK:]
        half[:, lanes] = jnp.where(zl == 0, low, high)
        zsend[:, lanes] = jnp.where(zl == 0, high, low).astype(BF)
        return carry

    lax.fori_loop(0, KC, add_up, 0)
    last = pltpu.make_async_remote_copy(
        zsend, zrecv, ps.at[2], ps.at[3], device_id=sdev(1 - zl, x), device_id_type=MESH)
    last.start()

    def expert_sums(blocks):
        rows = [blocks[:, :, :, 16 * q:16 * q + 16].reshape(1024, 128) for q in range(2)]
        total = jnp.dot(pick[...], jnp.concatenate(rows, axis=1), preferred_element_type=F32)
        return total[:, 0:128].reshape(16, 16, 128), total[:, 128:].reshape(16, 16, 128)

    g1[3]()
    for pair_of in range(3):
        sums = expert_sums(back1[:, :, :, 32 * pair_of:32 * pair_of + 32])
        for i in range(2):
            q = 2 * pair_of + i
            grad_out[:, 16 * (q % 3):16 * (q % 3) + 16, 128 * (q // 3):128 * (q // 3) + 128] = sums[i]
    last.wait()
    dx_out[...] = (half[...] + zrecv[...].astype(F32)).astype(BF)
    g2[3]()
    low, high = expert_sums(back2[...])
    grad_out[:, :, 256:] = unpack_tail(jnp.concatenate([low, high], axis=1))[:, :, 0:80]


def shards(tokens, route_weight, counts, pulled, weights, cotangent):
    vmem, smem = pl.BlockSpec(memory_space=pltpu.VMEM), pl.BlockSpec(memory_space=pltpu.SMEM)
    dma = pltpu.SemaphoreType.DMA
    lane = lax.broadcasted_iota(jnp.int32, (TOK, D + 128), 1)
    both = jnp.where(lane < D, jnp.pad(tokens, ((0, 0), (0, 128))), route_weight[:, None])
    def blocks_of(n):
        outer = [(NY, NZ), (NZ, NY), (NY, NZ), (NZ, NY), (NZ, NY, NC)]
        return [pltpu.VMEM(shape + (n, 128), BF) for shape in outer]

    sems = [dma((2, NY)), dma((2, NZ)), dma((2, 2 * NY)), dma((3,))]
    return pl.pallas_call(
        main_kernel,
        out_shape=[
            jax.ShapeDtypeStruct((CAP, COLS), BF),
            jax.ShapeDtypeStruct((TOK, D), BF),
            jax.ShapeDtypeStruct(weights.shape, F32),
        ],
        in_specs=[smem, smem, vmem, vmem, vmem],
        out_specs=[vmem, vmem, vmem],
        scratch_shapes=[
            pltpu.VMEM((16, 96, 128), BF),
            pltpu.VMEM((16, 32, 128), BF),
            *blocks_of(96),
            *blocks_of(32),
            pltpu.VMEM((KC, KW, 384), BF),
            *blocks_of(96),
            *blocks_of(32),
            pltpu.VMEM((TOK, D + 128), BF),
            pltpu.VMEM((NX, 2 * TOK, D + 128), BF),
            pltpu.VMEM((KC, CAP, KW), BF),
            pltpu.VMEM((KC, KW, CAP), BF),
            pltpu.VMEM((CAP, 128), F32),
            pltpu.VMEM((CAP, 384), F32),
            pltpu.VMEM((CAP, 384), F32),
            pltpu.VMEM((CAP, 384), BF),
            pltpu.VMEM((256, 1024), BF),
            pltpu.VMEM((NX, 2 * TOK, D), BF),
            pltpu.VMEM((2, 4, 2 * TOK, D), BF),
            pltpu.VMEM((TOK, D), BF),
            pltpu.VMEM((TOK, D), BF),
            pltpu.VMEM((TOK, D), F32),
            *sems, *sems, *sems, *sems,
            dma((4,)), dma((2, 8)), dma((2, 2, 4, 2)),
        ],
        compiler_params=pltpu.CompilerParams(
            collective_id=1, has_side_effects=True, vmem_limit_bytes=36 << 20),
        name="exchange_and_compute",
    )(pulled, counts, both, weights, cotangent)


def solution(mesh):
    in_specs = (
        P(("group", "shard"), None),
        P(("group", "shard")),
        P("group"),
        P(),
        P(None, "group", "shard"),
        P("group", "shard"),
    )
    out_specs = (P("group", "shard"), P(("group", "shard"), None), P(None, "group", "shard"))
    return jax.shard_map(shards, mesh=mesh, in_specs=in_specs, out_specs=out_specs, check_vma=False)
```
